32 devices in a mesh: grp: 2 (over y), ep: 4 (over z), tp: 2 (over x), sub: 2 (over core).
Axes of the slice: x: 2, y: 2, z: 4, core: 2. Of those that a mesh axis runs over, the one named last changes fastest.
Arguments:
- tokens: bfloat16 [1024, 4096], P(('grp', 'ep', 'sub'), 'tp'), parts along dimension 0, may hold values from -6 to 6
- expert_ids: int32 [1024, 2], P(('grp', 'ep', 'sub')), parts along dimension 0, may hold values from 0 to 7, all different within a row; in each aligned block of 64 rows (0 to 63, 64 to 127, ...) at most 48 rows name the same one
- gate_values: bfloat16 [1024, 2], P(('grp', 'ep', 'sub')), parts along dimension 0, may hold values from 0.099609375 to 1
- w_gate: bfloat16 [8, 4096, 1536], P(('ep', 'sub'), None, 'tp'), may hold values from -0.09375 to 0.09375
- w_up: bfloat16 [8, 4096, 1536], P(('ep', 'sub'), None, 'tp'), may hold values from -0.09375 to 0.09375
- w_down: bfloat16 [8, 1536, 4096], P(('ep', 'sub'), 'tp'), may hold values from -0.15625 to 0.15625
Outputs:
- mixed: bfloat16 [1024, 4096], P(('grp', 'ep', 'sub'), 'tp'), parts along dimension 0
The draws below stay inside these ranges and needn't reach their ends.
There are 2 independent parts, one for each index of `grp`. The reference program is written for one: setup_inputs(seed, part) draws one part's arguments, and reference() takes and returns one part's arrays. A program takes and returns all parts, laid end to end along the dimension named above; an argument that names none is the same for every part. Nothing has to cross between parts.
Inputs may be any that keep to these rules, and one draw needn't show every extreme that they name: `expert_ids`: within each aligned block of 64 rows no expert is named by more than 48 rows, a bound that some block reaches; a row names 2 different experts.
All inputs are finite; a program needn't handle non-finite values.
Results may differ from the reference program's by a relative error of at most 0.0058.
Values may be sent and summed in bfloat16 or wider, within the bound.
No kernel may reach another device: no remote copies, remote signals or barrier semaphores. Data moves between devices by JAX's collectives and lax.ppermute only.
A program may use at most 128 MiB of HBM per device.

```python
import math
import jax
import jax.numpy as jnp
import numpy as np
from jax import lax

D = 4096
FF = 1536
TOK_DEV = 64
EXPERTS = 8
TOP = 2
CAP = 48
TOKENS = 512
N_TP = 2


def levels(own_key, shape, cuts, least, largest):
    def one(axis_at, blocks):
        heights = jax.random.uniform(jax.random.fold_in(jax.random.fold_in(own_key, 6), axis_at), (blocks,), jnp.float32, least / len(cuts), largest / len(cuts))
        return jnp.repeat(jnp.exp(heights), shape[axis_at] // blocks).reshape((-1,) + (1,) * (len(shape) - axis_at - 1))

    level = one(*cuts[0])
    for cut in cuts[1:]:
        level = level * one(*cut)
    return level


def assign_block(stream_key, own, number, rows, amount, top, most, skew):
    order = jax.random.permutation(stream_key, amount)
    packed, usual = load_shares(amount, rows * top, most, skew, True), load_shares(amount, rows * top, most, skew, False)
    places = jnp.arange(amount)

    def named(tallies, turn):
        used = int((tallies > 0).sum())
        fixed = max(1, used // 4)
        moved = fixed + (places - fixed + turn * (used - fixed)) % max(1, amount - fixed)
        return jnp.zeros((amount,), jnp.int32).at[order[jnp.where(places < fixed, places, moved)]].set(jnp.asarray(tallies, jnp.int32))

    tallies = jnp.where(number % 4 == 0, named(packed, number // 4), named(usual, number - number // 4 - 1))
    mixed = jax.random.permutation(jax.random.fold_in(own, 3), amount)
    giver, taker = mixed[0:amount // 2 * 2:2], mixed[1:amount // 2 * 2:2]
    margin = jnp.minimum(tallies[giver] - 1, most - tallies[taker]) // 2
    margin = jnp.where((giver == order[0]) | (taker == order[0]) | (tallies[taker] == 0), 0, jnp.maximum(margin, 0))
    moved = jax.random.randint(jax.random.fold_in(own, 4), (amount // 2,), 0, 1 << 20) % (margin + 1)
    tallies = tallies.at[giver].add(-moved).at[taker].add(moved)
    labels = jnp.searchsorted(jnp.cumsum(tallies), jnp.arange(rows * top), side="right").astype(jnp.int32)
    listing = labels.reshape(top, rows).T
    listing = listing[jax.random.permutation(jax.random.fold_in(own, 1), rows)]
    turn = jax.random.randint(jax.random.fold_in(own, 2), (rows, 1), 0, top)
    return jnp.take_along_axis(listing, (jnp.arange(top)[None, :] + turn) % top, axis=1)


def load_shares(amount, total, bound, slope, full):
    weights = [(1 << 20) // math.isqrt(standing ** slope) + 1 for standing in range(1, amount + 1)]
    largest = bound if full else min(bound, max(-(-total // amount), total * weights[0] // sum(weights)))
    least = 1 if total - largest >= amount - 1 else 0
    holding, surplus = [largest] + [least] * (amount - 1), total - largest - least * (amount - 1)
    while surplus > 0:
        free = [i for i in range(1, amount) if holding[i] < largest] or [i for i in range(1, amount) if holding[i] < bound]
        pool, left = sum([weights[i] for i in free]), surplus
        for i in free:
            extra = min(bound - holding[i], max(1, left * weights[i] // pool), surplus)
            holding[i] = holding[i] + extra
            surplus = surplus - extra
    return np.array(holding)


def scatter_about(own_key, shape, deviation, reach, cuts=(), held_as=jnp.bfloat16):
    factor_of = levels(own_key, shape, cuts, -0.22, 0.18) if cuts else 1.0
    result = jax.random.normal(own_key, shape, jnp.float32) * deviation * factor_of
    return jnp.minimum(jnp.maximum(result, -reach), reach).astype(held_as)


def setup_inputs(seed: int = 0, part: int = 0) -> dict:
    seeds = jax.random.split(jax.random.key(seed), 7)
    part_splits = jax.random.split(jax.random.fold_in(seeds[6], part), 7)
    tokens = scatter_about(part_splits[0], (TOKENS, D), 1.0, 6.0, ((0, 8), (1, 2)))
    expert_ids_keys = jax.random.split(jax.random.fold_in(part_splits[1], 1), TOKENS // TOK_DEV)
    expert_ids_turns = jax.random.permutation(jax.random.fold_in(part_splits[1], 3), TOKENS // TOK_DEV)
    expert_ids = jax.vmap(lambda own, number: assign_block(jax.random.fold_in(part_splits[1], 2), own, number, TOK_DEV, EXPERTS, TOP, CAP, 2))(expert_ids_keys, expert_ids_turns).reshape((TOKENS, TOP))
    gate_values = jnp.clip(jnp.exp(math.log(1.0) - 2.306499 * jax.random.uniform(part_splits[2], (TOKENS, TOP), jnp.float32) ** levels(part_splits[2], (TOKENS, TOP), ((0, 8),), -0.2, 0.2)), 0.099609375, 1.0).astype(jnp.bfloat16)
    w_gate = scatter_about(seeds[3], (EXPERTS, D, FF), D ** -0.5, 0.09375, ((0, 8), (2, 2)))
    w_up = scatter_about(seeds[4], (EXPERTS, D, FF), D ** -0.5, 0.09375, ((0, 8), (2, 2)))
    w_down = scatter_about(seeds[5], (EXPERTS, FF, D), FF ** -0.5, 0.15625, ((0, 8), (1, 2)))
    return dict(tokens=tokens, expert_ids=expert_ids, gate_values=gate_values, w_gate=w_gate, w_up=w_up, w_down=w_down)


def positions(ids_block):
    flat_ids = ids_block.reshape(-1)
    one_hot = (flat_ids[:, None] == jnp.arange(EXPERTS, dtype=jnp.int32)[None, :]).astype(jnp.int32)
    earlier = jnp.cumsum(one_hot, axis=0) - one_hot
    slot_idx = jnp.sum(earlier * one_hot, axis=1)
    return (flat_ids * CAP + slot_idx).reshape(ids_block.shape).astype(jnp.int32)


def reference(tokens, expert_ids, gate_values, w_gate, w_up, w_down):
    block_count = TOKENS // TOK_DEV
    positions_all = jax.vmap(positions)(expert_ids.reshape(block_count, TOK_DEV, TOP))
    rows_in = tokens.reshape(block_count, TOK_DEV, D).astype(jnp.float32)
    gates = gate_values.reshape(block_count, TOK_DEV, TOP).astype(jnp.float32)
    lane_ids = jnp.arange(CAP, dtype=jnp.int32)
    group_width = FF // N_TP

    def one_expert(total, inputs):
        expert, gate_w, up_w, down_w = inputs
        lane_want = expert * CAP + lane_ids
        lane_hits = positions_all[:, None, :, :] == lane_want[None, :, None, None]
        pick_mat = jnp.any(lane_hits, axis=3).astype(jnp.float32)
        picked = jnp.einsum('bct,btd->bcd', pick_mat, rows_in, precision=lax.Precision.HIGHEST)
        picked = picked.astype(jnp.bfloat16).reshape(block_count * CAP, D)
        gate_act = jnp.dot(picked, gate_w, preferred_element_type=jnp.float32)
        up_act = jnp.dot(picked, up_w, preferred_element_type=jnp.float32)
        hidden = (jax.nn.silu(gate_act) * up_act).astype(jnp.bfloat16)
        grouped = hidden.reshape(block_count * CAP, N_TP, group_width).astype(jnp.float32)
        down_f = down_w.reshape(N_TP, group_width, D).astype(jnp.float32)
        partial_value = jnp.einsum('rjf,jfd->rjd', grouped, down_f, precision=lax.Precision.HIGHEST)
        partial_value = lax.optimization_barrier(partial_value.astype(jnp.bfloat16)).astype(jnp.float32)
        summed = jnp.sum(partial_value, axis=1).reshape(block_count, CAP, D)
        weight = jnp.sum(jnp.where(lane_hits, gates[:, None, :, :], jnp.float32(0.0)), axis=3)
        total = total + jnp.einsum('bct,bcd->btd', weight, summed, precision=lax.Precision.HIGHEST)
        return total, None

    start = jnp.zeros((block_count, TOK_DEV, D), jnp.float32)
    total, _ = lax.scan(one_expert, start, (jnp.arange(EXPERTS, dtype=jnp.int32), w_gate, w_up, w_down))
    return total.reshape(TOKENS, D).astype(jnp.bfloat16)
```

```python
import functools

import jax
import jax.numpy as jnp
from jax import lax
from jax.experimental import pallas as pl
from jax.experimental.pallas import tpu as pltpu
from jax.sharding import PartitionSpec as P

LANES = 128


def slot_positions(ids_block, experts, capacity):
    flat_ids = ids_block.reshape(-1)
    one_hot = (flat_ids[:, None] == jnp.arange(experts, dtype=jnp.int32)[None, :]).astype(jnp.int32)
    earlier = jnp.cumsum(one_hot, axis=0) - one_hot
    slot_idx = jnp.sum(earlier * one_hot, axis=1)
    return (flat_ids * capacity + slot_idx).reshape(ids_block.shape)


def by_slots(tokens, expert_ids, gate_values, w_gate, w_up, w_down):
    peer_count = lax.axis_size(("ep", "sub"))
    tok_rows = tokens.shape[0]
    top_count = expert_ids.shape[1]
    capacity = 3 * tok_rows * top_count // peer_count
    lane_total = peer_count * capacity
    own_positions = slot_positions(expert_ids, peer_count, capacity)
    lane_ids = jnp.arange(lane_total, dtype=jnp.int32)
    lane_hits = own_positions[None, :, :] == lane_ids[:, None, None]
    dispatch_mat = jnp.any(lane_hits, axis=2).astype(jnp.bfloat16)
    weight_back = jnp.sum(
        jnp.where(lane_hits, gate_values.astype(jnp.float32)[None, :, :], jnp.float32(0.0)), axis=2
    )
    combine_mat = weight_back.T.astype(jnp.bfloat16)
    full_rows = lax.all_gather(tokens, "tp", axis=1, tiled=True)
    outgoing = jnp.dot(dispatch_mat, full_rows, preferred_element_type=jnp.float32).astype(
        jnp.bfloat16
    )
    outgoing = outgoing.reshape(peer_count, capacity, full_rows.shape[1])
    arrived = lax.all_to_all(outgoing, ("ep", "sub"), split_axis=0, concat_axis=0, tiled=True)
    flat_rows = arrived.reshape(peer_count * capacity, arrived.shape[2])
    gate_act = jnp.dot(flat_rows, w_gate[0], preferred_element_type=jnp.float32)
    up_act = jnp.dot(flat_rows, w_up[0], preferred_element_type=jnp.float32)
    hidden = (jax.nn.silu(gate_act) * up_act).astype(jnp.bfloat16)
    partial_value = jnp.dot(hidden, w_down[0], preferred_element_type=jnp.float32).astype(
        jnp.bfloat16
    )
    partial_value = partial_value.reshape(peer_count, capacity, w_down.shape[2])
    returned = lax.all_to_all(partial_value, ("ep", "sub"), split_axis=0, concat_axis=0, tiled=True)
    local_sum = jnp.dot(
        combine_mat,
        returned.reshape(lane_total, returned.shape[2]),
        preferred_element_type=jnp.float32,
    )
    mixed = lax.psum_scatter(local_sum, "tp", scatter_dimension=1, tiled=True)
    return mixed.astype(jnp.bfloat16)


def expert_kernel(where_ref, own_ref, other_ref, gate_ref, up_ref, down_ref, out_ref, hidden_ref, scale_ref):
    half = gate_ref.shape[0] // 2
    rows = own_ref.shape[1]
    width = gate_ref.shape[1]
    tp, expert = where_ref[0], where_ref[1]
    mine = pl.ds(pl.multiple_of(tp * half, half), half)
    peers = pl.ds(pl.multiple_of((1 - tp) * half, half), half)
    sources = (own_ref, other_ref)
    tile = 256 if width % 256 == 0 else width
    lane = lax.broadcasted_iota(jnp.int32, (rows, LANES), 1)
    for s, source in enumerate(sources):
        weights = source[0, :, half:].astype(jnp.float32)
        scale_ref[s] = jnp.sum(jnp.where(lane == expert, weights, 0.0), axis=1, keepdims=True)

    @pl.loop(0, width // tile)
    def _(j):
        columns = pl.ds(pl.multiple_of(j * tile, tile), tile)
        for s, source in enumerate(sources):
            def act(weight_ref):
                return jnp.dot(
                    source[0, :, :half], weight_ref[mine, columns], preferred_element_type=jnp.float32
                ) + jnp.dot(
                    source[1, :, :half], weight_ref[peers, columns], preferred_element_type=jnp.float32
                )
            gate = act(gate_ref)
            hidden_ref[s, :, columns] = (gate / (1.0 + jnp.exp(-gate)) * act(up_ref)).astype(jnp.bfloat16)

    out_tile = 512
    for h in range(2):
        @pl.loop(0, half // out_tile)
        def _(n):
            to = pl.multiple_of(n * out_tile, out_tile)
            start = pl.multiple_of((tp if h == 0 else 1 - tp) * half + n * out_tile, out_tile)
            for s in range(2):
                value = jnp.dot(
                    hidden_ref[s], down_ref[:, pl.ds(start, out_tile)], preferred_element_type=jnp.float32
                )
                out_ref[s, h, :, pl.ds(to, out_tile)] = (value * scale_ref[s]).astype(jnp.bfloat16)


def run_expert(where, own, other, w_gate, w_up, w_down):
    rows, half = own.shape[1], w_gate.shape[0] // 2
    width = w_gate.shape[1]
    vmem = pl.BlockSpec(memory_space=pltpu.VMEM)
    return pl.pallas_call(
        expert_kernel,
        out_shape=jax.ShapeDtypeStruct((2, 2, rows, half), jnp.bfloat16),
        in_specs=[pl.BlockSpec(memory_space=pltpu.SMEM)] + [vmem] * 5,
        out_specs=vmem,
        scratch_shapes=[
            pltpu.VMEM((2, rows, width), jnp.bfloat16),
            pltpu.VMEM((2, rows, 1), jnp.float32),
        ],
        compiler_params=pltpu.CompilerParams(vmem_limit_bytes=48 * 1024 * 1024),
        cost_estimate=pl.CostEstimate(
            flops=2 * 2 * rows * 3 * 2 * half * width, bytes_accessed=3 * 2 * half * width * 2, transcendentals=0
        ),
    )(where, own, other, w_gate, w_up, w_down)


def by_rows(tokens, expert_ids, gate_values, w_gate, w_up, w_down):
    ep, sub = lax.axis_size("ep"), lax.axis_size("sub")
    rows, half = tokens.shape
    swap = [(0, 1), (1, 0)]
    ahead = lambda k: [(i, (i + k) % ep) for i in range(ep)]
    lanes = jnp.arange(LANES, dtype=jnp.int32)
    weights = jnp.sum(
        jnp.where(expert_ids[:, :, None] == lanes, gate_values.astype(jnp.float32)[:, :, None], 0.0), axis=1
    )
    packed = jnp.concatenate([tokens, weights.astype(jnp.bfloat16)], axis=1)
    mine = [packed] + [lax.ppermute(packed, "ep", ahead(k)) for k in range(1, ep)]
    peers = [lax.ppermute(a, "tp", swap) for a in mine]
    own = jnp.stack(mine + peers).reshape(2, ep * rows, half + LANES)
    other = lax.ppermute(own, "sub", swap)
    where = jnp.stack([lax.axis_index("tp"), lax.axis_index("ep") * sub + lax.axis_index("sub")]).astype(jnp.int32)
    out = run_expert(where, own, other, w_gate[0], w_up[0], w_down[0])
    crossed = lax.ppermute(out[1], "sub", swap)
    to_peer = out[0, 1].astype(jnp.float32) + crossed[1].astype(jnp.float32)
    to_peer = to_peer.astype(jnp.bfloat16).reshape(ep, rows, half)
    keep = out[0, 0].astype(jnp.float32) + crossed[0].astype(jnp.float32)
    keep = keep.reshape(ep, rows, half)
    total = None
    for k in range(ep):
        part = keep[k] + lax.ppermute(to_peer[k], "tp", swap).astype(jnp.float32)
        if k:
            part = lax.ppermute(part.astype(jnp.bfloat16), "ep", ahead(-k)).astype(jnp.float32)
        total = part if total is None else total + part
    return total.astype(jnp.bfloat16)


def solution(mesh):
    in_specs = (
        P(("grp", "ep", "sub"), "tp"),
        P(("grp", "ep", "sub"), None),
        P(("grp", "ep", "sub"), None),
        P(("ep", "sub"), None, "tp"),
        P(("ep", "sub"), None, "tp"),
        P(("ep", "sub"), "tp", None),
    )
    out_specs = P(("grp", "ep", "sub"), "tp")
    small = mesh.shape["tp"] == 2 and mesh.shape["sub"] == 2 and mesh.shape["ep"] <= 4
    return jax.shard_map(
        by_rows if small else by_slots, mesh=mesh, in_specs=in_specs, out_specs=out_specs, check_vma=False
    )
```

```python
import functools

import jax
import jax.numpy as jnp
from jax import lax
from jax.experimental import pallas as pl
from jax.experimental.pallas import tpu as pltpu
from jax.sharding import PartitionSpec as P

LANES = 128


def slot_positions(ids_block, experts, capacity):
    flat_ids = ids_block.reshape(-1)
    one_hot = (flat_ids[:, None] == jnp.arange(experts, dtype=jnp.int32)[None, :]).astype(jnp.int32)
    earlier = jnp.cumsum(one_hot, axis=0) - one_hot
    slot_idx = jnp.sum(earlier * one_hot, axis=1)
    return (flat_ids * capacity + slot_idx).reshape(ids_block.shape)


def by_slots(tokens, expert_ids, gate_values, w_gate, w_up, w_down):
    peer_count = lax.axis_size(("ep", "sub"))
    tok_rows = tokens.shape[0]
    top_count = expert_ids.shape[1]
    capacity = 3 * tok_rows * top_count // peer_count
    lane_total = peer_count * capacity
    own_positions = slot_positions(expert_ids, peer_count, capacity)
    lane_ids = jnp.arange(lane_total, dtype=jnp.int32)
    lane_hits = own_positions[None, :, :] == lane_ids[:, None, None]
    dispatch_mat = jnp.any(lane_hits, axis=2).astype(jnp.bfloat16)
    weight_back = jnp.sum(
        jnp.where(lane_hits, gate_values.astype(jnp.float32)[None, :, :], jnp.float32(0.0)), axis=2
    )
    combine_mat = weight_back.T.astype(jnp.bfloat16)
    full_rows = lax.all_gather(tokens, "tp", axis=1, tiled=True)
    outgoing = jnp.dot(dispatch_mat, full_rows, preferred_element_type=jnp.float32).astype(
        jnp.bfloat16
    )
    outgoing = outgoing.reshape(peer_count, capacity, full_rows.shape[1])
    arrived = lax.all_to_all(outgoing, ("ep", "sub"), split_axis=0, concat_axis=0, tiled=True)
    flat_rows = arrived.reshape(peer_count * capacity, arrived.shape[2])
    gate_act = jnp.dot(flat_rows, w_gate[0], preferred_element_type=jnp.float32)
    up_act = jnp.dot(flat_rows, w_up[0], preferred_element_type=jnp.float32)
    hidden = (jax.nn.silu(gate_act) * up_act).astype(jnp.bfloat16)
    partial_value = jnp.dot(hidden, w_down[0], preferred_element_type=jnp.float32).astype(
        jnp.bfloat16
    )
    partial_value = partial_value.reshape(peer_count, capacity, w_down.shape[2])
    returned = lax.all_to_all(partial_value, ("ep", "sub"), split_axis=0, concat_axis=0, tiled=True)
    local_sum = jnp.dot(
        combine_mat,
        returned.reshape(lane_total, returned.shape[2]),
        preferred_element_type=jnp.float32,
    )
    mixed = lax.psum_scatter(local_sum, "tp", scatter_dimension=1, tiled=True)
    return mixed.astype(jnp.bfloat16)


def expert_kernel(count, after, resident, where_ref, *refs):
    refs = refs[after:]
    pieces, refs = refs[: 4 * count], refs[4 * count:]
    if resident:
        gate_ref, up_ref, down_ref, mine_ref, cross_ref, x_ref, hidden_ref, scale_ref = refs
    else:
        from_refs, (mine_ref, cross_ref, gate_ref, up_ref, down_ref, x_ref, hidden_ref, scale_ref, sems) = refs[:3], refs[3:]
    depth, width = gate_ref.shape
    half = depth // 2
    rows = pieces[0].shape[0]
    tile = 256 if width % 256 == 0 else width
    tiles = width // tile
    down_parts = 4
    out_tile = depth // down_parts // 2
    tp, expert = where_ref[0], where_ref[1]
    starts = [pl.multiple_of(h * half, half) for h in (tp, 1 - tp)]
    copies = []
    if not resident:
        for j in range(tiles):
            columns = pl.ds(j * tile, tile)
            copies += [
                pltpu.make_async_copy(source.at[:, columns], target.at[:, columns], sems.at[2 * j + i])
                for i, (source, target) in enumerate(zip(from_refs[:2], (gate_ref, up_ref)))
            ]
        for i in range(down_parts):
            h = i // (down_parts // 2)
            columns = pl.ds(pl.multiple_of(starts[1 - h] + (i % (down_parts // 2)) * 2 * out_tile, out_tile), 2 * out_tile)
            copies.append(
                pltpu.make_async_copy(from_refs[2].at[:, columns], down_ref.at[:, columns], sems.at[2 * tiles + i])
            )
        for copy in copies:
            copy.start()
    lane = lax.broadcasted_iota(jnp.int32, (rows, LANES), 1)
    for at in range(2 * count):
        row = pl.ds(at * rows, rows)
        own, peer = pieces[2 * at], pieces[2 * at + 1]
        weights = own[:, half:].astype(jnp.float32)
        scale_ref[row, :] = jnp.sum(jnp.where(lane == expert, weights, 0.0), axis=1, keepdims=True)
        x_ref[row, pl.ds(starts[0], half)] = own[:, :half]
        x_ref[row, pl.ds(starts[1], half)] = peer[:, :half]

    for j in range(tiles):
        columns = pl.ds(j * tile, tile)
        for copy in copies[2 * j: 2 * j + 2]:
            copy.wait()
        gate = jnp.dot(x_ref[...], gate_ref[:, columns], preferred_element_type=jnp.float32)
        up = jnp.dot(x_ref[...], up_ref[:, columns], preferred_element_type=jnp.float32)
        hidden_ref[:, columns] = (gate / (1.0 + jnp.exp(-gate)) * up).astype(jnp.bfloat16)

    part = count * rows
    for i in range(down_parts):
        h = 1 - i // (down_parts // 2)
        for copy in copies[2 * tiles + i: 2 * tiles + i + 1]:
            copy.wait()
        for n in range(2):
            offset = (i % (down_parts // 2)) * 2 * out_tile + n * out_tile
            start = pl.multiple_of(starts[h] + offset, out_tile)
            value = jnp.dot(
                hidden_ref[...], down_ref[:, pl.ds(start, out_tile)], preferred_element_type=jnp.float32
            ) * scale_ref[...]
            mine_ref[h, :, pl.ds(offset, out_tile)] = value[:part]
            cross_ref[h, :, pl.ds(offset, out_tile)] = value[part:].astype(jnp.bfloat16)


def run_expert(where, after, pieces, weights, resident):
    count = len(pieces) // 4
    rows, (depth, width) = pieces[0].shape[0], weights[0].shape
    half = depth // 2
    vmem = pl.BlockSpec(memory_space=pltpu.VMEM)
    hbm = pl.BlockSpec(memory_space=pltpu.HBM)
    held = [] if resident else [pltpu.VMEM(a.shape, a.dtype) for a in weights]
    if not resident:
        weights = [pltpu.with_memory_space_constraint(a, pltpu.HBM) for a in weights]
    return pl.pallas_call(
        functools.partial(expert_kernel, count, len(after), resident),
        out_shape=[
            pltpu.VMEM((2, count * rows, half), jnp.float32),
            pltpu.VMEM((2, count * rows, half), jnp.bfloat16),
        ] + held,
        in_specs=[pl.BlockSpec(memory_space=pltpu.SMEM)]
        + [pl.BlockSpec(memory_space=pl.ANY)] * len(after)
        + [vmem] * len(pieces) + [vmem if resident else hbm] * 3,
        out_specs=[vmem] * (2 + len(held)),
        scratch_shapes=[
            pltpu.VMEM((2 * count * rows, depth), jnp.bfloat16),
            pltpu.VMEM((2 * count * rows, width), jnp.bfloat16),
            pltpu.VMEM((2 * count * rows, 1), jnp.float32),
        ] + ([] if resident else [pltpu.SemaphoreType.DMA((2 * max(1, width // 256) + 4,))]),
        compiler_params=pltpu.CompilerParams(vmem_limit_bytes=12 * 1024 * 1024),
        cost_estimate=pl.CostEstimate(
            flops=2 * 2 * count * rows * 3 * depth * width,
            bytes_accessed=1024 if resident else 3 * depth * width * 2,
            transcendentals=0,
        ),
    )(where, *after, *pieces, *weights)


def by_rows(tokens, expert_ids, gate_values, w_gate, w_up, w_down):
    ep, sub = lax.axis_size("ep"), lax.axis_size("sub")
    rows, half = tokens.shape
    swap = [(0, 1), (1, 0)]
    ahead = lambda k: [(i, (i + k) % ep) for i in range(ep)]
    lanes = jnp.arange(LANES, dtype=jnp.int32)
    weights = jnp.sum(
        jnp.where(expert_ids[:, :, None] == lanes, gate_values.astype(jnp.float32)[:, :, None], 0.0), axis=1
    )
    packed = jnp.concatenate([tokens, weights.astype(jnp.bfloat16)], axis=1)
    where = jnp.stack([lax.axis_index("tp"), lax.axis_index("ep") * sub + lax.axis_index("sub")]).astype(jnp.int32)
    mine = [packed] + [lax.ppermute(packed, "ep", ahead(k)) for k in range(1, ep)]
    peers = [lax.ppermute(a, "tp", swap) for a in mine]
    order = sorted(range(ep), key=lambda k: min(k, ep - k))
    first = ep // 2
    held, resident, after, total = [w_gate[0], w_up[0], w_down[0]], False, mine[1:] + peers[ep // 2 + 1:], None
    for group in (order[:first], order[first:]):
        own = [a for k in group for a in (mine[k], peers[k])]
        other = [lax.ppermute(a, "sub", swap) for a in own]
        result, crossing, *rest = run_expert(where, after, own + other, held, resident)
        held, resident = (held, True) if resident else (rest, True)
        crossed = lax.ppermute(crossing, "sub", swap)
        after = []
        for i, k in reversed(list(enumerate(group))):
            at = slice(i * rows, (i + 1) * rows)
            to_peer = (result[1, at] + crossed[1, at].astype(jnp.float32)).astype(jnp.bfloat16)
            part = result[0, at] + crossed[0, at].astype(jnp.float32)
            part = part + lax.ppermute(to_peer, "tp", swap).astype(jnp.float32)
            after.append(to_peer)
            if k:
                part = lax.ppermute(part.astype(jnp.bfloat16), "ep", ahead(-k)).astype(jnp.float32)
            total = part if total is None else total + part
    return total.astype(jnp.bfloat16)


def solution(mesh):
    in_specs = (
        P(("grp", "ep", "sub"), "tp"),
        P(("grp", "ep", "sub"), None),
        P(("grp", "ep", "sub"), None),
        P(("ep", "sub"), None, "tp"),
        P(("ep", "sub"), None, "tp"),
        P(("ep", "sub"), "tp", None),
    )
    out_specs = P(("grp", "ep", "sub"), "tp")
    small = mesh.shape["tp"] == 2 and mesh.shape["sub"] == 2 and mesh.shape["ep"] <= 4
    return jax.shard_map(
        by_rows if small else by_slots, mesh=mesh, in_specs=in_specs, out_specs=out_specs, check_vma=False
    )
```

```python
import functools

import jax
import jax.numpy as jnp
from jax import lax
from jax.experimental import pallas as pl
from jax.experimental.pallas import tpu as pltpu
from jax.sharding import PartitionSpec as P

LANES = 128


def slot_positions(ids_block, experts, capacity):
    flat_ids = ids_block.reshape(-1)
    one_hot = (flat_ids[:, None] == jnp.arange(experts, dtype=jnp.int32)[None, :]).astype(jnp.int32)
    earlier = jnp.cumsum(one_hot, axis=0) - one_hot
    slot_idx = jnp.sum(earlier * one_hot, axis=1)
    return (flat_ids * capacity + slot_idx).reshape(ids_block.shape)


def by_slots(tokens, expert_ids, gate_values, w_gate, w_up, w_down):
    peer_count = lax.axis_size(("ep", "sub"))
    tok_rows = tokens.shape[0]
    top_count = expert_ids.shape[1]
    capacity = 3 * tok_rows * top_count // peer_count
    lane_total = peer_count * capacity
    own_positions = slot_positions(expert_ids, peer_count, capacity)
    lane_ids = jnp.arange(lane_total, dtype=jnp.int32)
    lane_hits = own_positions[None, :, :] == lane_ids[:, None, None]
    dispatch_mat = jnp.any(lane_hits, axis=2).astype(jnp.bfloat16)
    weight_back = jnp.sum(
        jnp.where(lane_hits, gate_values.astype(jnp.float32)[None, :, :], jnp.float32(0.0)), axis=2
    )
    combine_mat = weight_back.T.astype(jnp.bfloat16)
    full_rows = lax.all_gather(tokens, "tp", axis=1, tiled=True)
    outgoing = jnp.dot(dispatch_mat, full_rows, preferred_element_type=jnp.float32).astype(
        jnp.bfloat16
    )
    outgoing = outgoing.reshape(peer_count, capacity, full_rows.shape[1])
    arrived = lax.all_to_all(outgoing, ("ep", "sub"), split_axis=0, concat_axis=0, tiled=True)
    flat_rows = arrived.reshape(peer_count * capacity, arrived.shape[2])
    gate_act = jnp.dot(flat_rows, w_gate[0], preferred_element_type=jnp.float32)
    up_act = jnp.dot(flat_rows, w_up[0], preferred_element_type=jnp.float32)
    hidden = (jax.nn.silu(gate_act) * up_act).astype(jnp.bfloat16)
    partial_value = jnp.dot(hidden, w_down[0], preferred_element_type=jnp.float32).astype(
        jnp.bfloat16
    )
    partial_value = partial_value.reshape(peer_count, capacity, w_down.shape[2])
    returned = lax.all_to_all(partial_value, ("ep", "sub"), split_axis=0, concat_axis=0, tiled=True)
    local_sum = jnp.dot(
        combine_mat,
        returned.reshape(lane_total, returned.shape[2]),
        preferred_element_type=jnp.float32,
    )
    mixed = lax.psum_scatter(local_sum, "tp", scatter_dimension=1, tiled=True)
    return mixed.astype(jnp.bfloat16)


def pack_kernel(tokens_ref, ids_hbm_ref, gates_hbm_ref, out_ref, ids_ref, gates_ref, sems):
    rows, half = tokens_ref.shape
    copies = [
        pltpu.make_async_copy(source, target, sems.at[i])
        for i, (source, target) in enumerate(
            ((ids_hbm_ref, ids_ref), (gates_hbm_ref, gates_ref), (tokens_ref, out_ref.at[:, pl.ds(0, half)]))
        )
    ]
    for copy in copies:
        copy.start()
    for copy in copies[:2]:
        copy.wait()
    expert = lax.broadcasted_iota(jnp.int32, (LANES, rows), 0)
    weights = jnp.zeros((LANES, rows), jnp.float32)
    for k in range(ids_ref.shape[0]):
        weights = weights + jnp.where(expert == ids_ref[k:k + 1, :], gates_ref[k:k + 1, :].astype(jnp.float32), 0.0)
    out_ref[:, half:] = weights.T.astype(jnp.bfloat16)
    copies[2].wait()


def pack(tokens, expert_ids, gate_values):
    arrays = [pltpu.with_memory_space_constraint(a, pltpu.HBM) for a in (tokens, expert_ids.T, gate_values.T)]
    return pl.pallas_call(
        pack_kernel,
        out_shape=pltpu.VMEM((tokens.shape[0], tokens.shape[1] + LANES), jnp.bfloat16),
        in_specs=[pl.BlockSpec(memory_space=pltpu.HBM)] * 3,
        out_specs=pl.BlockSpec(memory_space=pltpu.VMEM),
        scratch_shapes=[pltpu.VMEM(a.shape, a.dtype) for a in arrays[1:]] + [pltpu.SemaphoreType.DMA((3,))],
        compiler_params=pltpu.CompilerParams(vmem_limit_bytes=1024 * 1024),
    )(*arrays)


def expert_kernel(count, after, resident, where_ref, *refs):
    refs = refs[after:]
    pieces, refs = refs[: 4 * count], refs[4 * count:]
    if resident:
        gate_ref, up_ref, down_ref, mine_ref, cross_ref, x_ref, hidden_ref, scale_ref = refs
    else:
        from_refs, (mine_ref, cross_ref, gate_ref, up_ref, down_ref, x_ref, hidden_ref, scale_ref, sems) = refs[:3], refs[3:]
    depth, width = gate_ref.shape
    half = depth // 2
    rows = pieces[0].shape[0]
    tile = 256 if width % 256 == 0 else width
    tiles = width // tile
    down_parts = 4
    out_tile = depth // down_parts // 2
    tp, expert = where_ref[0], where_ref[1]
    starts = [pl.multiple_of(h * half, half) for h in (tp, 1 - tp)]
    copies = []
    if not resident:
        for j in range(tiles):
            columns = pl.ds(j * tile, tile)
            copies += [
                pltpu.make_async_copy(source.at[:, columns], target.at[:, columns], sems.at[2 * j + i])
                for i, (source, target) in enumerate(zip(from_refs[:2], (gate_ref, up_ref)))
            ]
        for i in range(down_parts):
            h = i // (down_parts // 2)
            columns = pl.ds(pl.multiple_of(starts[1 - h] + (i % (down_parts // 2)) * 2 * out_tile, out_tile), 2 * out_tile)
            copies.append(
                pltpu.make_async_copy(from_refs[2].at[:, columns], down_ref.at[:, columns], sems.at[2 * tiles + i])
            )
        for copy in copies:
            copy.start()
    lane = lax.broadcasted_iota(jnp.int32, (rows, LANES), 1)
    for at in range(2 * count):
        row = pl.ds(at * rows, rows)
        own, peer = pieces[2 * at], pieces[2 * at + 1]
        weights = own[:, half:].astype(jnp.float32)
        scale_ref[row, :] = jnp.sum(jnp.where(lane == expert, weights, 0.0), axis=1, keepdims=True)
        x_ref[row, pl.ds(starts[0], half)] = own[:, :half]
        x_ref[row, pl.ds(starts[1], half)] = peer[:, :half]

    for j in range(tiles):
        columns = pl.ds(j * tile, tile)
        for copy in copies[2 * j: 2 * j + 2]:
            copy.wait()
        gate = jnp.dot(x_ref[...], gate_ref[:, columns], preferred_element_type=jnp.float32)
        up = jnp.dot(x_ref[...], up_ref[:, columns], preferred_element_type=jnp.float32)
        hidden_ref[:, columns] = (gate / (1.0 + jnp.exp(-gate)) * up).astype(jnp.bfloat16)

    part = count * rows
    for i in range(down_parts):
        h = 1 - i // (down_parts // 2)
        for copy in copies[2 * tiles + i: 2 * tiles + i + 1]:
            copy.wait()
        for n in range(2):
            offset = (i % (down_parts // 2)) * 2 * out_tile + n * out_tile
            start = pl.multiple_of(starts[h] + offset, out_tile)
            value = jnp.dot(
                hidden_ref[...], down_ref[:, pl.ds(start, out_tile)], preferred_element_type=jnp.float32
            ) * scale_ref[...]
            mine_ref[h, :, pl.ds(offset, out_tile)] = value[:part]
            cross_ref[h, :, pl.ds(offset, out_tile)] = value[part:].astype(jnp.bfloat16)


def run_expert(where, after, pieces, weights, resident):
    count = len(pieces) // 4
    rows, (depth, width) = pieces[0].shape[0], weights[0].shape
    half = depth // 2
    vmem = pl.BlockSpec(memory_space=pltpu.VMEM)
    hbm = pl.BlockSpec(memory_space=pltpu.HBM)
    held = [] if resident else [pltpu.VMEM(a.shape, a.dtype) for a in weights]
    if not resident:
        weights = [pltpu.with_memory_space_constraint(a, pltpu.HBM) for a in weights]
    return pl.pallas_call(
        functools.partial(expert_kernel, count, len(after), resident),
        out_shape=[
            pltpu.VMEM((2, count * rows, half), jnp.float32),
            pltpu.VMEM((2, count * rows, half), jnp.bfloat16),
        ] + held,
        in_specs=[pl.BlockSpec(memory_space=pltpu.SMEM)]
        + [pl.BlockSpec(memory_space=pl.ANY)] * len(after)
        + [vmem] * len(pieces) + [vmem if resident else hbm] * 3,
        out_specs=[vmem] * (2 + len(held)),
        scratch_shapes=[
            pltpu.VMEM((2 * count * rows, depth), jnp.bfloat16),
            pltpu.VMEM((2 * count * rows, width), jnp.bfloat16),
            pltpu.VMEM((2 * count * rows, 1), jnp.float32),
        ] + ([] if resident else [pltpu.SemaphoreType.DMA((2 * max(1, width // 256) + 4,))]),
        compiler_params=pltpu.CompilerParams(vmem_limit_bytes=12 * 1024 * 1024),
        cost_estimate=pl.CostEstimate(
            flops=2 * 2 * count * rows * 3 * depth * width,
            bytes_accessed=1024 if resident else 3 * depth * width * 2,
            transcendentals=0,
        ),
    )(where, *after, *pieces, *weights)


def add_kernel(h, at, rows, *refs):
    *refs, result_ref, crossed_ref, out_ref = refs
    row = pl.ds(at * rows, rows)
    total = result_ref[h, row, :] + crossed_ref[h, row, :].astype(jnp.float32)
    for ref in refs:
        total = total + ref[...].astype(jnp.float32)
    out_ref[...] = total.astype(out_ref.dtype)


def add(h, at, rows, result, crossed, *arrived):
    vmem = pl.BlockSpec(memory_space=pltpu.VMEM)
    return pl.pallas_call(
        functools.partial(add_kernel, h, at, rows),
        out_shape=pltpu.VMEM((rows, result.shape[2]), jnp.bfloat16),
        in_specs=[vmem] * (2 + len(arrived)),
        out_specs=vmem,
        compiler_params=pltpu.CompilerParams(vmem_limit_bytes=4 * 1024 * 1024),
        cost_estimate=pl.CostEstimate(flops=0, bytes_accessed=1024, transcendentals=0),
    )(*arrived, result, crossed)


def tie_kernel(*refs):
    pass


def tie_all(arrays, *after):
    count = len(arrays)
    return pl.pallas_call(
        tie_kernel,
        out_shape=[pltpu.VMEM(a.shape, a.dtype) for a in arrays],
        in_specs=[pl.BlockSpec(memory_space=pltpu.VMEM)] * count + [pl.BlockSpec(memory_space=pl.ANY)] * len(after),
        out_specs=[pl.BlockSpec(memory_space=pltpu.VMEM)] * count,
        input_output_aliases={i: i for i in range(count)},
        compiler_params=pltpu.CompilerParams(vmem_limit_bytes=1024 * 1024),
        cost_estimate=pl.CostEstimate(flops=0, bytes_accessed=0, transcendentals=0),
    )(*arrays, *after)


def tie(array, *after):
    return tie_all([array], *after)[0]


def by_rows(tokens, expert_ids, gate_values, w_gate, w_up, w_down):
    ep = lax.axis_size("ep")
    rows = tokens.shape[0]
    swap = [(0, 1), (1, 0)]
    ahead = lambda k: [(i, (i + k) % ep) for i in range(ep)]
    far = ep // 2
    second = tuple(k for k in range(1, ep) if k != far)
    packed = pack(tokens, expert_ids, gate_values)
    mine = {k: lax.ppermute(packed, "ep", ahead(k)) if k else packed for k in (far, *second, 0)}
    where = jnp.stack([lax.axis_index("tp"), lax.axis_index("ep") * 2 + lax.axis_index("sub")]).astype(jnp.int32)
    peers = {0: lax.ppermute(packed, "tp", swap)}

    def multiply(group, after, weights, resident=True):
        own = [a for k in group for a in (mine[k], peers[k])]
        other = [lax.ppermute(a, "sub", swap) for a in own]
        return run_expert(where, after, own + other, weights, resident)

    result, crossing, *weights = multiply((0,), [], [w_gate[0], w_up[0], w_down[0]], False)
    here = result, lax.ppermute(crossing, "sub", swap)
    peers |= {k: lax.ppermute(mine[k], "tp", swap) for k in (far, *second)}
    peers[far] = tie(peers[far], crossing, mine[second[0]])
    result, crossing = multiply((far,), [mine[k] for k in second], weights)
    crossing = tie(crossing, peers[second[0]])
    later = result, lax.ppermute(crossing, "sub", swap)
    to_peer = add(1, 0, rows, *later)
    arrived = lax.ppermute(to_peer, "tp", swap)
    result, crossing = multiply(second, [to_peer], weights)
    crossing = tie(crossing, arrived)
    sums = [lax.ppermute(add(0, 0, rows, *later, arrived), "ep", ahead(-far))]
    crossed = lax.ppermute(crossing, "sub", swap)
    to_peer = [add(1, i, rows, result, crossed) for i in range(len(second))]
    arrived = [lax.ppermute(a, "tp", swap) for a in to_peer]
    sums += [
        lax.ppermute(add(0, i, rows, result, crossed, arrived[i]), "ep", ahead(-k)) for i, k in enumerate(second)
    ]
    last = lax.ppermute(tie(add(1, 0, rows, *here), *to_peer), "tp", swap)
    total = here[0][0] + here[1][0].astype(jnp.float32)
    for a in (last, *sums):
        total = total + a.astype(jnp.float32)
    return total.astype(jnp.bfloat16)


def solution(mesh):
    in_specs = (
        P(("grp", "ep", "sub"), "tp"),
        P(("grp", "ep", "sub"), None),
        P(("grp", "ep", "sub"), None),
        P(("ep", "sub"), None, "tp"),
        P(("ep", "sub"), None, "tp"),
        P(("ep", "sub"), "tp", None),
    )
    out_specs = P(("grp", "ep", "sub"), "tp")
    small = mesh.shape["tp"] == 2 and mesh.shape["sub"] == 2 and mesh.shape["ep"] == 4
    return jax.shard_map(
        by_rows if small else by_slots, mesh=mesh, in_specs=in_specs, out_specs=out_specs, check_vma=False
    )
```

```python
import functools

import jax
import jax.numpy as jnp
from jax import lax
from jax.experimental import pallas as pl
from jax.experimental.pallas import tpu as pltpu
from jax.sharding import PartitionSpec as P

LANES = 128


def slot_positions(ids_block, experts, capacity):
    flat_ids = ids_block.reshape(-1)
    one_hot = (flat_ids[:, None] == jnp.arange(experts, dtype=jnp.int32)[None, :]).astype(jnp.int32)
    earlier = jnp.cumsum(one_hot, axis=0) - one_hot
    slot_idx = jnp.sum(earlier * one_hot, axis=1)
    return (flat_ids * capacity + slot_idx).reshape(ids_block.shape)


def by_slots(tokens, expert_ids, gate_values, w_gate, w_up, w_down):
    peer_count = lax.axis_size(("ep", "sub"))
    tok_rows = tokens.shape[0]
    top_count = expert_ids.shape[1]
    capacity = 3 * tok_rows * top_count // peer_count
    lane_total = peer_count * capacity
    own_positions = slot_positions(expert_ids, peer_count, capacity)
    lane_ids = jnp.arange(lane_total, dtype=jnp.int32)
    lane_hits = own_positions[None, :, :] == lane_ids[:, None, None]
    dispatch_mat = jnp.any(lane_hits, axis=2).astype(jnp.bfloat16)
    weight_back = jnp.sum(
        jnp.where(lane_hits, gate_values.astype(jnp.float32)[None, :, :], jnp.float32(0.0)), axis=2
    )
    combine_mat = weight_back.T.astype(jnp.bfloat16)
    full_rows = lax.all_gather(tokens, "tp", axis=1, tiled=True)
    outgoing = jnp.dot(dispatch_mat, full_rows, preferred_element_type=jnp.float32).astype(
        jnp.bfloat16
    )
    outgoing = outgoing.reshape(peer_count, capacity, full_rows.shape[1])
    arrived = lax.all_to_all(outgoing, ("ep", "sub"), split_axis=0, concat_axis=0, tiled=True)
    flat_rows = arrived.reshape(peer_count * capacity, arrived.shape[2])
    gate_act = jnp.dot(flat_rows, w_gate[0], preferred_element_type=jnp.float32)
    up_act = jnp.dot(flat_rows, w_up[0], preferred_element_type=jnp.float32)
    hidden = (jax.nn.silu(gate_act) * up_act).astype(jnp.bfloat16)
    partial_value = jnp.dot(hidden, w_down[0], preferred_element_type=jnp.float32).astype(
        jnp.bfloat16
    )
    partial_value = partial_value.reshape(peer_count, capacity, w_down.shape[2])
    returned = lax.all_to_all(partial_value, ("ep", "sub"), split_axis=0, concat_axis=0, tiled=True)
    local_sum = jnp.dot(
        combine_mat,
        returned.reshape(lane_total, returned.shape[2]),
        preferred_element_type=jnp.float32,
    )
    mixed = lax.psum_scatter(local_sum, "tp", scatter_dimension=1, tiled=True)
    return mixed.astype(jnp.bfloat16)


def pack_kernel(tokens_ref, ids_hbm_ref, gates_hbm_ref, out_ref, ids_ref, gates_ref, sems):
    rows, half = tokens_ref.shape
    copies = [
        pltpu.make_async_copy(source, target, sems.at[i])
        for i, (source, target) in enumerate(
            ((ids_hbm_ref, ids_ref), (gates_hbm_ref, gates_ref), (tokens_ref, out_ref.at[:, pl.ds(0, half)]))
        )
    ]
    for copy in copies:
        copy.start()
    for copy in copies[:2]:
        copy.wait()
    expert = lax.broadcasted_iota(jnp.int32, (LANES, rows), 0)
    weights = jnp.zeros((LANES, rows), jnp.float32)
    for k in range(ids_ref.shape[0]):
        weights = weights + jnp.where(expert == ids_ref[k:k + 1, :], gates_ref[k:k + 1, :].astype(jnp.float32), 0.0)
    out_ref[:, half:] = weights.T.astype(jnp.bfloat16)
    copies[2].wait()


def pack(tokens, expert_ids, gate_values):
    arrays = [pltpu.with_memory_space_constraint(a, pltpu.HBM) for a in (tokens, expert_ids.T, gate_values.T)]
    return pl.pallas_call(
        pack_kernel,
        out_shape=pltpu.VMEM((tokens.shape[0], tokens.shape[1] + LANES), jnp.bfloat16),
        in_specs=[pl.BlockSpec(memory_space=pltpu.HBM)] * 3,
        out_specs=pl.BlockSpec(memory_space=pltpu.VMEM),
        scratch_shapes=[pltpu.VMEM(a.shape, a.dtype) for a in arrays[1:]] + [pltpu.SemaphoreType.DMA((3,))],
        compiler_params=pltpu.CompilerParams(vmem_limit_bytes=1024 * 1024),
    )(*arrays)


def expert_kernel(count, after, resident, where_ref, *refs):
    refs = refs[after:]
    pieces, refs = refs[: 4 * count], refs[4 * count:]
    if resident:
        gate_ref, up_ref, down_ref, mine_ref, cross_ref, x_ref, hidden_ref, scale_ref = refs
    else:
        from_refs, (mine_ref, cross_ref, gate_ref, up_ref, down_ref, x_ref, hidden_ref, scale_ref, sems) = refs[:3], refs[3:]
    depth, width = gate_ref.shape
    half = depth // 2
    rows = pieces[0].shape[0]
    tile = 256 if width % 256 == 0 else width
    tiles = width // tile
    down_parts = 4
    out_tile = depth // down_parts // 2
    tp, expert = where_ref[0], where_ref[1]
    starts = [pl.multiple_of(h * half, half) for h in (tp, 1 - tp)]
    copies = []
    if not resident:
        for j in range(tiles):
            columns = pl.ds(j * tile, tile)
            copies += [
                pltpu.make_async_copy(source.at[:, columns], target.at[:, columns], sems.at[2 * j + i])
                for i, (source, target) in enumerate(zip(from_refs[:2], (gate_ref, up_ref)))
            ]
        for i in range(down_parts):
            h = i // (down_parts // 2)
            columns = pl.ds(pl.multiple_of(starts[1 - h] + (i % (down_parts // 2)) * 2 * out_tile, out_tile), 2 * out_tile)
            copies.append(
                pltpu.make_async_copy(from_refs[2].at[:, columns], down_ref.at[:, columns], sems.at[2 * tiles + i])
            )
        for copy in copies:
            copy.start()
    lane = lax.broadcasted_iota(jnp.int32, (rows, LANES), 1)
    for at in range(2 * count):
        row = pl.ds(at * rows, rows)
        own, peer = pieces[2 * at], pieces[2 * at + 1]
        weights = own[:, half:].astype(jnp.float32)
        scale_ref[row, :] = jnp.sum(jnp.where(lane == expert, weights, 0.0), axis=1, keepdims=True)
        x_ref[row, pl.ds(starts[0], half)] = own[:, :half]
        x_ref[row, pl.ds(starts[1], half)] = peer[:, :half]

    for j in range(tiles):
        columns = pl.ds(j * tile, tile)
        for copy in copies[2 * j: 2 * j + 2]:
            copy.wait()
        gate = jnp.dot(x_ref[...], gate_ref[:, columns], preferred_element_type=jnp.float32)
        up = jnp.dot(x_ref[...], up_ref[:, columns], preferred_element_type=jnp.float32)
        hidden_ref[:, columns] = (gate / (1.0 + jnp.exp(-gate)) * up).astype(jnp.bfloat16)

    part = count * rows
    for i in range(down_parts):
        h = 1 - i // (down_parts // 2)
        for copy in copies[2 * tiles + i: 2 * tiles + i + 1]:
            copy.wait()
        for n in range(2):
            offset = (i % (down_parts // 2)) * 2 * out_tile + n * out_tile
            start = pl.multiple_of(starts[h] + offset, out_tile)
            value = jnp.dot(
                hidden_ref[...], down_ref[:, pl.ds(start, out_tile)], preferred_element_type=jnp.float32
            ) * scale_ref[...]
            mine_ref[h, :, pl.ds(offset, out_tile)] = value[:part]
            cross_ref[h, :, pl.ds(offset, out_tile)] = value[part:].astype(jnp.bfloat16)


def run_expert(where, after, pieces, weights, resident):
    count = len(pieces) // 4
    rows, (depth, width) = pieces[0].shape[0], weights[0].shape
    half = depth // 2
    vmem = pl.BlockSpec(memory_space=pltpu.VMEM)
    hbm = pl.BlockSpec(memory_space=pltpu.HBM)
    held = [] if resident else [pltpu.VMEM(a.shape, a.dtype) for a in weights]
    if not resident:
        weights = [pltpu.with_memory_space_constraint(a, pltpu.HBM) for a in weights]
    return pl.pallas_call(
        functools.partial(expert_kernel, count, len(after), resident),
        out_shape=[
            pltpu.VMEM((2, count * rows, half), jnp.float32),
            pltpu.VMEM((2, count * rows, half), jnp.bfloat16),
        ] + held,
        in_specs=[pl.BlockSpec(memory_space=pltpu.SMEM)]
        + [pl.BlockSpec(memory_space=pl.ANY)] * len(after)
        + [vmem] * len(pieces) + [vmem if resident else hbm] * 3,
        out_specs=[vmem] * (2 + len(held)),
        scratch_shapes=[
            pltpu.VMEM((2 * count * rows, depth), jnp.bfloat16),
            pltpu.VMEM((2 * count * rows, width), jnp.bfloat16),
            pltpu.VMEM((2 * count * rows, 1), jnp.float32),
        ] + ([] if resident else [pltpu.SemaphoreType.DMA((2 * max(1, width // 256) + 4,))]),
        compiler_params=pltpu.CompilerParams(vmem_limit_bytes=12 * 1024 * 1024),
        cost_estimate=pl.CostEstimate(
            flops=2 * 2 * count * rows * 3 * depth * width,
            bytes_accessed=1024 if resident else 3 * depth * width * 2,
            transcendentals=0,
        ),
    )(where, *after, *pieces, *weights)


def add_kernel(h, at, rows, *refs):
    *refs, result_ref, crossed_ref, out_ref = refs
    row = pl.ds(at * rows, rows)
    total = result_ref[h, row, :] + crossed_ref[h, row, :].astype(jnp.float32)
    for ref in refs:
        total = total + ref[...].astype(jnp.float32)
    out_ref[...] = total.astype(out_ref.dtype)


def add(h, at, rows, result, crossed, *arrived):
    vmem = pl.BlockSpec(memory_space=pltpu.VMEM)
    return pl.pallas_call(
        functools.partial(add_kernel, h, at, rows),
        out_shape=pltpu.VMEM((rows, result.shape[2]), jnp.bfloat16),
        in_specs=[vmem] * (2 + len(arrived)),
        out_specs=vmem,
        compiler_params=pltpu.CompilerParams(vmem_limit_bytes=4 * 1024 * 1024),
        cost_estimate=pl.CostEstimate(flops=0, bytes_accessed=1024, transcendentals=0),
    )(*arrived, result, crossed)


def tie_kernel(*refs):
    pass


def tie_all(arrays, *after):
    count = len(arrays)
    return pl.pallas_call(
        tie_kernel,
        out_shape=[pltpu.VMEM(a.shape, a.dtype) for a in arrays],
        in_specs=[pl.BlockSpec(memory_space=pltpu.VMEM)] * count + [pl.BlockSpec(memory_space=pl.ANY)] * len(after),
        out_specs=[pl.BlockSpec(memory_space=pltpu.VMEM)] * count,
        input_output_aliases={i: i for i in range(count)},
        compiler_params=pltpu.CompilerParams(vmem_limit_bytes=1024 * 1024),
        cost_estimate=pl.CostEstimate(flops=0, bytes_accessed=0, transcendentals=0),
    )(*arrays, *after)


def tie(array, *after):
    return tie_all([array], *after)[0]


def by_rows(tokens, expert_ids, gate_values, w_gate, w_up, w_down):
    ep = lax.axis_size("ep")
    rows = tokens.shape[0]
    swap = [(0, 1), (1, 0)]
    across = lambda k: [(i, i ^ k) for i in range(ep)]
    far = ep // 2
    second = (far + 1, far - 1)
    packed = pack(tokens, expert_ids, gate_values)
    mine = {k: lax.ppermute(packed, "ep", across(k)) if k else packed for k in (far, *second, 0)}
    where = jnp.stack([lax.axis_index("tp"), lax.axis_index("ep") * 2 + lax.axis_index("sub")]).astype(jnp.int32)
    peers = {0: lax.ppermute(packed, "tp", swap)}

    def multiply(group, after, weights, resident=True):
        own = [a for k in group for a in (mine[k], peers[k])]
        other = [lax.ppermute(a, "sub", swap) for a in own]
        return run_expert(where, after, own + other, weights, resident)

    result, crossing, *weights = multiply((0,), [], [w_gate[0], w_up[0], w_down[0]], False)
    here = result, lax.ppermute(crossing, "sub", swap)
    peers |= {k: lax.ppermute(mine[k], "tp", swap) for k in (far, *second)}
    peers[far] = tie(peers[far], crossing, mine[second[1]])
    result, crossing = multiply((far,), [mine[k] for k in second], weights)
    crossing = tie(crossing, peers[second[0]])
    later = result, lax.ppermute(crossing, "sub", swap)
    to_peer = add(1, 0, rows, *later)
    passed = add(0, 0, rows, *later, lax.ppermute(to_peer, "tp", swap))
    result, crossing = multiply(second, [to_peer], weights)
    crossed = lax.ppermute(tie(crossing, passed), "sub", swap)
    passed = lax.ppermute(passed, "ep", across(far ^ second[0]))
    to_peer = [add(1, i, rows, result, crossed) for i in range(len(second))]
    arrived = [lax.ppermute(a, "tp", swap) for a in to_peer]
    last = lax.ppermute(tie(add(1, 0, rows, *here), *to_peer), "tp", swap)
    sums = [
        lax.ppermute(add(0, 0, rows, result, crossed, arrived[0], passed), "ep", across(second[0])),
        lax.ppermute(add(0, 1, rows, result, crossed, arrived[1]), "ep", across(second[1])),
    ]
    total = here[0][0] + here[1][0].astype(jnp.float32)
    for a in (last, *sums):
        total = total + a.astype(jnp.float32)
    return total.astype(jnp.bfloat16)


def solution(mesh):
    in_specs = (
        P(("grp", "ep", "sub"), "tp"),
        P(("grp", "ep", "sub"), None),
        P(("grp", "ep", "sub"), None),
        P(("ep", "sub"), None, "tp"),
        P(("ep", "sub"), None, "tp"),
        P(("ep", "sub"), "tp", None),
    )
    out_specs = P(("grp", "ep", "sub"), "tp")
    small = mesh.shape["tp"] == 2 and mesh.shape["sub"] == 2 and mesh.shape["ep"] == 4
    return jax.shard_map(
        by_rows if small else by_slots, mesh=mesh, in_specs=in_specs, out_specs=out_specs, check_vma=False
    )
```

```python
import functools

import jax
import jax.numpy as jnp
from jax import lax
from jax.experimental import pallas as pl
from jax.experimental.pallas import tpu as pltpu
from jax.sharding import PartitionSpec as P

LANES = 128


def slot_positions(ids_block, experts, capacity):
    flat_ids = ids_block.reshape(-1)
    one_hot = (flat_ids[:, None] == jnp.arange(experts, dtype=jnp.int32)[None, :]).astype(jnp.int32)
    earlier = jnp.cumsum(one_hot, axis=0) - one_hot
    slot_idx = jnp.sum(earlier * one_hot, axis=1)
    return (flat_ids * capacity + slot_idx).reshape(ids_block.shape)


def by_slots(tokens, expert_ids, gate_values, w_gate, w_up, w_down):
    peer_count = lax.axis_size(("ep", "sub"))
    tok_rows = tokens.shape[0]
    top_count = expert_ids.shape[1]
    capacity = 3 * tok_rows * top_count // peer_count
    lane_total = peer_count * capacity
    own_positions = slot_positions(expert_ids, peer_count, capacity)
    lane_ids = jnp.arange(lane_total, dtype=jnp.int32)
    lane_hits = own_positions[None, :, :] == lane_ids[:, None, None]
    dispatch_mat = jnp.any(lane_hits, axis=2).astype(jnp.bfloat16)
    weight_back = jnp.sum(
        jnp.where(lane_hits, gate_values.astype(jnp.float32)[None, :, :], jnp.float32(0.0)), axis=2
    )
    combine_mat = weight_back.T.astype(jnp.bfloat16)
    full_rows = lax.all_gather(tokens, "tp", axis=1, tiled=True)
    outgoing = jnp.dot(dispatch_mat, full_rows, preferred_element_type=jnp.float32).astype(
        jnp.bfloat16
    )
    outgoing = outgoing.reshape(peer_count, capacity, full_rows.shape[1])
    arrived = lax.all_to_all(outgoing, ("ep", "sub"), split_axis=0, concat_axis=0, tiled=True)
    flat_rows = arrived.reshape(peer_count * capacity, arrived.shape[2])
    gate_act = jnp.dot(flat_rows, w_gate[0], preferred_element_type=jnp.float32)
    up_act = jnp.dot(flat_rows, w_up[0], preferred_element_type=jnp.float32)
    hidden = (jax.nn.silu(gate_act) * up_act).astype(jnp.bfloat16)
    partial_value = jnp.dot(hidden, w_down[0], preferred_element_type=jnp.float32).astype(
        jnp.bfloat16
    )
    partial_value = partial_value.reshape(peer_count, capacity, w_down.shape[2])
    returned = lax.all_to_all(partial_value, ("ep", "sub"), split_axis=0, concat_axis=0, tiled=True)
    local_sum = jnp.dot(
        combine_mat,
        returned.reshape(lane_total, returned.shape[2]),
        preferred_element_type=jnp.float32,
    )
    mixed = lax.psum_scatter(local_sum, "tp", scatter_dimension=1, tiled=True)
    return mixed.astype(jnp.bfloat16)


def pack_kernel(tokens_ref, ids_hbm_ref, gates_hbm_ref, out_ref, ids_ref, gates_ref, sems):
    rows, half = tokens_ref.shape
    copies = [
        pltpu.make_async_copy(source, target, sems.at[i])
        for i, (source, target) in enumerate(
            ((ids_hbm_ref, ids_ref), (gates_hbm_ref, gates_ref), (tokens_ref, out_ref.at[:, pl.ds(0, half)]))
        )
    ]
    for copy in copies:
        copy.start()
    for copy in copies[:2]:
        copy.wait()
    expert = lax.broadcasted_iota(jnp.int32, (LANES, rows), 0)
    weights = jnp.zeros((LANES, rows), jnp.float32)
    for k in range(ids_ref.shape[0]):
        weights = weights + jnp.where(expert == ids_ref[k:k + 1, :], gates_ref[k:k + 1, :].astype(jnp.float32), 0.0)
    out_ref[:, half:] = weights.T.astype(jnp.bfloat16)
    copies[2].wait()


def pack(tokens, expert_ids, gate_values):
    arrays = [pltpu.with_memory_space_constraint(a, pltpu.HBM) for a in (tokens, expert_ids.T, gate_values.T)]
    return pl.pallas_call(
        pack_kernel,
        out_shape=pltpu.VMEM((tokens.shape[0], tokens.shape[1] + LANES), jnp.bfloat16),
        in_specs=[pl.BlockSpec(memory_space=pltpu.HBM)] * 3,
        out_specs=pl.BlockSpec(memory_space=pltpu.VMEM),
        scratch_shapes=[pltpu.VMEM(a.shape, a.dtype) for a in arrays[1:]] + [pltpu.SemaphoreType.DMA((3,))],
        compiler_params=pltpu.CompilerParams(vmem_limit_bytes=1024 * 1024),
    )(*arrays)


def expert_kernel(count, after, resident, where_ref, *refs):
    refs = refs[after:]
    pieces, refs = refs[: 4 * count], refs[4 * count:]
    if resident:
        gate_ref, up_ref, down_ref, mine_ref, cross_ref, x_ref, hidden_ref, scale_ref = refs
    else:
        from_refs, (mine_ref, cross_ref, gate_ref, up_ref, down_ref, x_ref, hidden_ref, scale_ref, sems) = refs[:3], refs[3:]
    depth, width = gate_ref.shape
    half = depth // 2
    rows = pieces[0].shape[0]
    tile = 256 if width % 256 == 0 else width
    tiles = width // tile
    down_parts = 4
    out_tile = depth // down_parts // 2
    tp, expert = where_ref[0], where_ref[1]
    starts = [pl.multiple_of(h * half, half) for h in (tp, 1 - tp)]
    copies = []
    if not resident:
        for j in range(tiles):
            columns = pl.ds(j * tile, tile)
            copies += [
                pltpu.make_async_copy(source.at[:, columns], target.at[:, columns], sems.at[2 * j + i])
                for i, (source, target) in enumerate(zip(from_refs[:2], (gate_ref, up_ref)))
            ]
        for i in range(down_parts):
            h = i // (down_parts // 2)
            columns = pl.ds(pl.multiple_of(starts[1 - h] + (i % (down_parts // 2)) * 2 * out_tile, out_tile), 2 * out_tile)
            copies.append(
                pltpu.make_async_copy(from_refs[2].at[:, columns], down_ref.at[:, columns], sems.at[2 * tiles + i])
            )
        for copy in copies:
            copy.start()
    lane = lax.broadcasted_iota(jnp.int32, (rows, LANES), 1)
    for at in range(2 * count):
        row = pl.ds(at * rows, rows)
        own, peer = pieces[2 * at], pieces[2 * at + 1]
        weights = own[:, half:].astype(jnp.float32)
        scale_ref[row, :] = jnp.sum(jnp.where(lane == expert, weights, 0.0), axis=1, keepdims=True)
        x_ref[row, pl.ds(starts[0], half)] = own[:, :half]
        x_ref[row, pl.ds(starts[1], half)] = peer[:, :half]

    for j in range(tiles):
        columns = pl.ds(j * tile, tile)
        for copy in copies[2 * j: 2 * j + 2]:
            copy.wait()
        gate = jnp.dot(x_ref[...], gate_ref[:, columns], preferred_element_type=jnp.float32)
        up = jnp.dot(x_ref[...], up_ref[:, columns], preferred_element_type=jnp.float32)
        hidden_ref[:, columns] = (gate / (1.0 + jnp.exp(-gate)) * up).astype(jnp.bfloat16)

    part = count * rows
    for i in range(down_parts):
        h = 1 - i // (down_parts // 2)
        for copy in copies[2 * tiles + i: 2 * tiles + i + 1]:
            copy.wait()
        for n in range(2):
            offset = (i % (down_parts // 2)) * 2 * out_tile + n * out_tile
            start = pl.multiple_of(starts[h] + offset, out_tile)
            value = jnp.dot(
                hidden_ref[...], down_ref[:, pl.ds(start, out_tile)], preferred_element_type=jnp.float32
            ) * scale_ref[...]
            mine_ref[h, :, pl.ds(offset, out_tile)] = value[:part]
            cross_ref[h, :, pl.ds(offset, out_tile)] = value[part:].astype(jnp.bfloat16)


def run_expert(where, after, pieces, weights, resident):
    count = len(pieces) // 4
    rows, (depth, width) = pieces[0].shape[0], weights[0].shape
    half = depth // 2
    vmem = pl.BlockSpec(memory_space=pltpu.VMEM)
    hbm = pl.BlockSpec(memory_space=pltpu.HBM)
    held = [] if resident else [pltpu.VMEM(a.shape, a.dtype) for a in weights]
    if not resident:
        weights = [pltpu.with_memory_space_constraint(a, pltpu.HBM) for a in weights]
    return pl.pallas_call(
        functools.partial(expert_kernel, count, len(after), resident),
        out_shape=[
            pltpu.VMEM((2, count * rows, half), jnp.float32),
            pltpu.VMEM((2, count * rows, half), jnp.bfloat16),
        ] + held,
        in_specs=[pl.BlockSpec(memory_space=pltpu.SMEM)]
        + [pl.BlockSpec(memory_space=pl.ANY)] * len(after)
        + [vmem] * len(pieces) + [vmem if resident else hbm] * 3,
        out_specs=[vmem] * (2 + len(held)),
        scratch_shapes=[
            pltpu.VMEM((2 * count * rows, depth), jnp.bfloat16),
            pltpu.VMEM((2 * count * rows, width), jnp.bfloat16),
            pltpu.VMEM((2 * count * rows, 1), jnp.float32),
        ] + ([] if resident else [pltpu.SemaphoreType.DMA((2 * max(1, width // 256) + 4,))]),
        compiler_params=pltpu.CompilerParams(vmem_limit_bytes=12 * 1024 * 1024),
        cost_estimate=pl.CostEstimate(
            flops=2 * 2 * count * rows * 3 * depth * width,
            bytes_accessed=1024 if resident else 3 * depth * width * 2,
            transcendentals=0,
        ),
    )(where, *after, *pieces, *weights)


def add_kernel(h, at, rows, *refs):
    *refs, result_ref, crossed_ref, out_ref = refs
    row = pl.ds(at * rows, rows)
    total = result_ref[h, row, :] + crossed_ref[h, row, :].astype(jnp.float32)
    for ref in refs:
        total = total + ref[...].astype(jnp.float32)
    out_ref[...] = total.astype(out_ref.dtype)


def add(h, at, rows, result, crossed, *arrived):
    vmem = pl.BlockSpec(memory_space=pltpu.VMEM)
    return pl.pallas_call(
        functools.partial(add_kernel, h, at, rows),
        out_shape=pltpu.VMEM((rows, result.shape[2]), jnp.bfloat16),
        in_specs=[vmem] * (2 + len(arrived)),
        out_specs=vmem,
        compiler_params=pltpu.CompilerParams(vmem_limit_bytes=4 * 1024 * 1024),
        cost_estimate=pl.CostEstimate(flops=0, bytes_accessed=1024, transcendentals=0),
    )(*arrived, result, crossed)


def tie_kernel(*refs):
    pass


def tie_all(arrays, *after):
    count = len(arrays)
    return pl.pallas_call(
        tie_kernel,
        out_shape=[pltpu.VMEM(a.shape, a.dtype) for a in arrays],
        in_specs=[pl.BlockSpec(memory_space=pltpu.VMEM)] * count + [pl.BlockSpec(memory_space=pl.ANY)] * len(after),
        out_specs=[pl.BlockSpec(memory_space=pltpu.VMEM)] * count,
        input_output_aliases={i: i for i in range(count)},
        compiler_params=pltpu.CompilerParams(vmem_limit_bytes=1024 * 1024),
        cost_estimate=pl.CostEstimate(flops=0, bytes_accessed=0, transcendentals=0),
    )(*arrays, *after)


def tie(array, *after):
    return tie_all([array], *after)[0]


def by_rows(tokens, expert_ids, gate_values, w_gate, w_up, w_down):
    ep = lax.axis_size("ep")
    rows = tokens.shape[0]
    swap = [(0, 1), (1, 0)]
    across = lambda k: [(i, i ^ k) for i in range(ep)]
    far = ep // 2
    second = (far + 1, far - 1)
    packed = pack(tokens, expert_ids, gate_values)
    mine = {k: lax.ppermute(packed, "ep", across(k)) if k else packed for k in (far, *second, 0)}
    where = jnp.stack([lax.axis_index("tp"), lax.axis_index("ep") * 2 + lax.axis_index("sub")]).astype(jnp.int32)
    peers = {0: lax.ppermute(packed, "tp", swap)}

    def multiply(group, after, weights, resident=True):
        own = [a for k in group for a in (mine[k], peers[k])]
        other = [lax.ppermute(a, "sub", swap) for a in own]
        return run_expert(where, after, own + other, weights, resident)

    result, crossing, *weights = multiply((0,), [], [w_gate[0], w_up[0], w_down[0]], False)
    here = result, lax.ppermute(crossing, "sub", swap)
    peers |= {k: lax.ppermute(mine[k], "tp", swap) for k in (far, *second)}
    peers[far] = tie(peers[far], crossing, peers[second[1]])
    result, crossing = multiply((far,), [mine[k] for k in second], weights)
    later = result, lax.ppermute(crossing, "sub", swap)
    to_peer = add(1, 0, rows, *later)
    passed = add(0, 0, rows, *later, lax.ppermute(to_peer, "tp", swap))
    result, crossing = multiply(second, [to_peer], weights)
    crossed = lax.ppermute(tie(crossing, passed), "sub", swap)
    passed = lax.ppermute(passed, "ep", across(far ^ second[0]))
    to_peer = [add(1, i, rows, result, crossed) for i in range(len(second))]
    arrived = [lax.ppermute(a, "tp", swap) for a in to_peer]
    last = lax.ppermute(tie(add(1, 0, rows, *here), *to_peer), "tp", swap)
    sums = [
        lax.ppermute(add(0, 0, rows, result, crossed, arrived[0], passed), "ep", across(second[0])),
        lax.ppermute(add(0, 1, rows, result, crossed, arrived[1]), "ep", across(second[1])),
    ]
    total = here[0][0] + here[1][0].astype(jnp.float32)
    for a in (last, *sums):
        total = total + a.astype(jnp.float32)
    return total.astype(jnp.bfloat16)


def solution(mesh):
    in_specs = (
        P(("grp", "ep", "sub"), "tp"),
        P(("grp", "ep", "sub"), None),
        P(("grp", "ep", "sub"), None),
        P(("ep", "sub"), None, "tp"),
        P(("ep", "sub"), None, "tp"),
        P(("ep", "sub"), "tp", None),
    )
    out_specs = P(("grp", "ep", "sub"), "tp")
    small = mesh.shape["tp"] == 2 and mesh.shape["sub"] == 2 and mesh.shape["ep"] == 4
    return jax.shard_map(
        by_rows if small else by_slots, mesh=mesh, in_specs=in_specs, out_specs=out_specs, check_vma=False
    )
```
